512 devices in a mesh: rep: 32 (over y, z_lo), tp: 16 (over z_hi, x, core).
Axes of the slice: x: 4, y: 4, z: 16 (z_hi: 2, z_lo: 8; z = z_hi * 8 + z_lo), core: 2. Of those that a mesh axis runs over, the one named last changes fastest.
Arguments:
- hidden: bfloat16 [14336, 7168], P('rep', 'tp'), may hold values from -6 to 6
- upstream: bfloat16 [14336, 2048], P('rep', 'tp'), may hold values from -6 to 6
- weights: bfloat16 [7168, 8192], P('tp', 'rep'), may hold values from -2 to 2
- first_moment: float32 [7168, 8192], P('tp', 'rep'), may hold values from -0.12 to 0.12
- second_moment: float32 [7168, 8192], P('tp', 'rep'), may hold values from 1e-06 to 0.001
- step_index: int32 [1], replicated, may hold values from 0 to 63
Outputs:
- mixed_weights: bfloat16 [7168, 8192], P('tp', 'rep')
- new_first: float32 [7168, 8192], P('tp', 'rep')
- new_second: float32 [7168, 8192], P('tp', 'rep')
- hidden_grad: bfloat16 [14336, 7168], P('rep', 'tp')
The draws below stay inside these ranges and needn't reach their ends.
All inputs are finite; a program needn't handle non-finite values.
Results may differ from the reference program's by a relative error of at most 0.0052.
Values may be sent and summed in bfloat16 or wider, within the bound.
No kernel may reach another device: no remote copies, remote signals or barrier semaphores. Data moves between devices by JAX's collectives and lax.ppermute only.
A program may use at most 64 MiB of HBM per device.

```python
import math
import jax
import jax.numpy as jnp
from jax import lax

D = 2048
HID = 448
TOK = 448
REPLICAS = 4
SPLIT = 8
FF = 7168
N_REP = 32


def block_scale(key, dims, shards, least, largest):
    level = 1.0
    for axis_at, blocks in shards:
        heights = jax.random.uniform(jax.random.fold_in(jax.random.fold_in(key, 6), axis_at), (blocks,), jnp.float32, least / len(shards), largest / len(shards))
        level = level * jnp.repeat(jnp.exp(heights), dims[axis_at] // blocks).reshape((-1,) + (1,) * (len(dims) - 1 - axis_at))
    return level


def normal_values(key, dims, width, most, cuts=(), kind=jnp.bfloat16):
    values = width * jax.random.normal(key, dims, jnp.float32)
    if cuts:
        values = values * block_scale(key, dims, cuts, -0.22, 0.18)
    return jnp.clip(values, -most, most).astype(kind)


def setup_inputs(seed: int = 0) -> dict:
    arg_keys = jax.random.split(jax.random.key(seed), 7)
    return {
        "hidden": normal_values(arg_keys[0], (N_REP * TOK, FF), 1.0, 6.0, ((0, 32), (1, 16))),
        "upstream": normal_values(arg_keys[1], (N_REP * TOK, D), 1.0, 6.0, ((0, 32), (1, 16))),
        "weights": normal_values(arg_keys[2], (FF, REPLICAS * D), 0.5, 2.0, ((0, 16), (1, 32))),
        "first_moment": normal_values(arg_keys[3], (FF, REPLICAS * D), 0.02, 0.12, ((0, 16), (1, 32)), jnp.float32),
        "second_moment": jnp.clip(jnp.exp(math.log(0.001) - 6.9077553 * jax.random.uniform(arg_keys[4], (FF, REPLICAS * D), jnp.float32) ** block_scale(arg_keys[4], (FF, REPLICAS * D), ((0, 16), (1, 32)), -0.2, 0.2)), 9.999999974752427e-07, 0.001),
        "step_index": jax.random.randint(arg_keys[5], (1,), 0, 64).astype(jnp.int32),
    }


def replica_step(packed):
    hid, ups, weights, first_moment, second_moment, count = packed
    scale_hid = 1.0 / math.sqrt(FF)
    grads = jnp.dot(hid.T, ups, preferred_element_type=jnp.float32) * scale_hid
    in_grad = (jnp.dot(ups, weights.T, preferred_element_type=jnp.float32) * scale_hid).astype(jnp.bfloat16)
    first_new = 0.9 * first_moment + 0.1 * grads
    second_new = 0.999 * second_moment + 0.001 * grads * grads
    correct_one = 1.0 - jnp.power(jnp.float32(0.9), count)
    correct_two = 1.0 - jnp.power(jnp.float32(0.999), count)
    weights_f = weights.astype(jnp.float32)
    step_size = first_new / correct_one / (jnp.sqrt(second_new / correct_two) + 1e-08) + 0.1 * weights_f
    updated = (weights_f - 0.05 * step_size).astype(jnp.bfloat16)
    return (updated, first_new, second_new, in_grad)

def by_replica(array):
    return jnp.transpose(array.reshape(FF, REPLICAS, D), (1, 0, 2))

def by_column(array):
    return jnp.transpose(array, (1, 0, 2)).reshape(FF, REPLICAS * D)

def reference(hidden, upstream, weights, first_moment, second_moment, step_index):
    count = (step_index[0] + 1).astype(jnp.float32)
    counts = jnp.zeros((REPLICAS,), jnp.float32) + count
    hid = hidden.reshape(REPLICAS, SPLIT * TOK, FF)
    ups = upstream.reshape(REPLICAS, SPLIT * TOK, D)
    updated, first_new, second_new, in_grad = lax.map(replica_step, (hid, ups, by_replica(weights), by_replica(first_moment), by_replica(second_moment), counts))
    unit_rows = jnp.arange(FF, dtype=jnp.int32)
    bucket = (unit_rows % HID >= HID // 2).astype(jnp.int32)
    near_rows = (step_index[0].astype(jnp.int32) + bucket) % 2 == 0
    partner = jnp.where(near_rows[None, :, None], jnp.roll(updated, 1, axis=0), jnp.roll(updated, 2, axis=0))
    mixed = ((updated.astype(jnp.float32) + partner.astype(jnp.float32)) * 0.5).astype(jnp.bfloat16)
    return (by_column(mixed), by_column(first_new), by_column(second_new), in_grad.reshape(REPLICAS * SPLIT * TOK, FF))
```

```python
import math

import jax
import jax.numpy as jnp
from jax import lax
from jax.sharding import Mesh, PartitionSpec as P

BF = jnp.bfloat16
F32 = jnp.float32
LINE = 8
LEAD = 1


def swap_cores(value):
    return lax.ppermute(value, "c", [(0, 1), (1, 0)])


def hop(value, odd):
    pairs = []
    for chip in range(LINE - 1):
        low, high = chip * 2 + odd, (chip + 1) * 2 + 1 - odd
        pairs += [(low, high), (high, low)]
    return lax.ppermute(value, ("zl", "c"), pairs)


def contract(left, right, dims):
    return lax.dot_general(left, right, (dims, ((), ())), preferred_element_type=F32)


def body(hidden, upstream, weights, first_moment, second_moment, step_index):
    tokens, units = hidden.shape
    width = weights.shape[1]
    place, core, far_half = lax.axis_index("zl"), lax.axis_index("c"), lax.axis_index("zh")
    first_core = core == 0
    scale_hid = 1.0 / math.sqrt(7168)

    weights_other = swap_cores(weights)
    both_weights = jnp.where(
        first_core,
        jnp.concatenate([weights, weights_other], 0),
        jnp.concatenate([weights_other, weights], 0),
    )
    hidden_other = swap_cores(hidden)
    both_hidden = jnp.where(
        first_core,
        jnp.concatenate([hidden, hidden_other], 1),
        jnp.concatenate([hidden_other, hidden], 1),
    )

    up_other = lax.ppermute(upstream, "zh", [(0, 1), (1, 0)])
    near_up = lax.all_gather(upstream, ("x", "c"), axis=1, tiled=True)
    far_up = lax.all_gather(up_other, ("x", "c"), axis=1, tiled=True)
    full_up = jnp.concatenate([near_up, far_up], axis=1)

    def up_block(index):
        at = jnp.bitwise_xor(index, 4 * far_half) * width
        return lax.dynamic_slice_in_dim(full_up, at, width, 1)

    carried = both_weights
    hg_total = jnp.zeros((tokens, 2 * units), F32)
    for step in range(LINE - 1 + LEAD):
        upward = core == step % 2
        turn = step - LEAD
        payload = carried
        if turn >= 0:
            position = jnp.where(upward, place, LINE - 1 - place)
            block = jnp.clip(LINE - 1 - turn + position, 0, LINE - 1)
            block = jnp.where(upward, block, LINE - 1 - block)
            part = contract(both_hidden, up_block(block), ((0,), (0,)))
            part = lax.optimization_barrier(part)
            payload = jnp.where(position <= turn, (carried.astype(F32) + part).astype(BF), carried)
        carried = hop(payload, step % 2)
        if step < LINE - 1:
            position = jnp.where(upward, LINE - 1 - place, place)
            source = position - 1 - step
            valid = source >= 0
            source = jnp.clip(source, 0, LINE - 1)
            source = jnp.where(upward, LINE - 1 - source, source)
            features = jnp.where(valid, up_block(source), jnp.zeros((), BF))
            hg_total = hg_total + contract(features, carried, ((1,), (1,)))

    own_up = up_block(place)
    mine = lax.dynamic_slice_in_dim(carried, core * units, units, 0)
    theirs = lax.dynamic_slice_in_dim(carried, (1 - core) * units, units, 0)
    own_part = contract(hidden, own_up, ((0,), (0,)))
    grads = (mine.astype(F32) + own_part + swap_cores(theirs).astype(F32)) * scale_hid

    count = (step_index[0] + 1).astype(F32)
    first_new = 0.9 * first_moment + 0.1 * grads
    second_new = 0.999 * second_moment + 0.001 * grads * grads
    correct_one = 1.0 - jnp.power(F32(0.9), count)
    correct_two = 1.0 - jnp.power(F32(0.999), count)
    weights_f = weights.astype(F32)
    step_size = first_new / correct_one / (jnp.sqrt(second_new / correct_two) + 1e-08) + 0.1 * weights_f
    updated = (weights_f - 0.05 * step_size).astype(BF)

    half = units // 2
    even_step = step_index[0] % 2 == 0
    lower, upper = updated[:half], updated[half:]
    near = lax.ppermute(jnp.where(even_step, lower, upper), "y", [(i, (i + 1) % 4) for i in range(4)])
    far = lax.ppermute(jnp.where(even_step, upper, lower), "y", [(i, (i + 2) % 4) for i in range(4)])
    partner = jnp.concatenate([jnp.where(even_step, near, far), jnp.where(even_step, far, near)], 0)
    mixed = ((updated.astype(F32) + partner.astype(F32)) * 0.5).astype(BF)

    hg_mine = lax.dynamic_slice_in_dim(hg_total, core * units, units, 1)
    hg_theirs = lax.dynamic_slice_in_dim(hg_total, (1 - core) * units, units, 1)
    hg_own = contract(own_up, weights, ((1,), (1,)))
    in_grad = ((hg_mine + hg_own + swap_cores(hg_theirs)) * scale_hid).astype(BF)
    return mixed, first_new, second_new, in_grad


def solution(mesh):
    split = Mesh(mesh.devices.reshape(4, LINE, 2, 4, 2), ("y", "zl", "zh", "x", "c"))
    rep, tp = ("y", "zl"), ("zh", "x", "c")
    in_specs = (P(rep, tp), P(rep, tp), P(tp, rep), P(tp, rep), P(tp, rep), P())
    out_specs = (P(tp, rep), P(tp, rep), P(tp, rep), P(rep, tp))
    return jax.shard_map(body, mesh=split, in_specs=in_specs, out_specs=out_specs, check_vma=False)
```

```python
import math

import jax
import jax.numpy as jnp
from jax import lax
from jax.sharding import Mesh, PartitionSpec as P

BF = jnp.bfloat16
F32 = jnp.float32
LINE = 8
LEAD = 1


def along(value, way):
    return lax.ppermute(value, "zl", [(i, i + way) for i in range(LINE) if 0 <= i + way < LINE])


def contract(left, right, dims):
    return lax.dot_general(left, right, (dims, ((), ())), preferred_element_type=F32)


def after(value, other):
    mark = other[0, 0]
    return jnp.where(mark != mark, jnp.zeros((), value.dtype), value)


def body(hidden, upstream, weights, first_moment, second_moment, step_index):
    width = weights.shape[1]
    place, far_half = lax.axis_index("zl"), lax.axis_index("zh")
    scale_hid = 1.0 / math.sqrt(7168)

    up_other = lax.ppermute(upstream, "zh", [(0, 1), (1, 0)])
    near_up = lax.all_gather(upstream, ("x", "c"), axis=1, tiled=True)
    far_up = lax.all_gather(up_other, ("x", "c"), axis=1, tiled=True)
    full_up = jnp.concatenate([near_up, far_up], axis=1)
    hidden_t = lax.optimization_barrier(hidden.T)

    def up_block(index):
        at = jnp.bitwise_xor(index, 4 * far_half) * width
        return lax.dynamic_slice_in_dim(full_up, at, width, 1)

    own_up = up_block(place)
    hg_total = contract(own_up, weights, ((1,), (1,)))
    start = after(weights, near_up)
    carried = {1: start, -1: start}
    for step in range(LINE - 1 + LEAD):
        turn = step - LEAD
        for way in (1, -1):
            position = place if way == 1 else LINE - 1 - place
            payload = carried[way]
            if turn >= 0:
                block = jnp.clip(LINE - 1 - turn + position, 0, LINE - 1)
                block = block if way == 1 else LINE - 1 - block
                part = lax.optimization_barrier(contract(hidden_t, up_block(block), ((1,), (0,))))
                payload = jnp.where(position <= turn, (payload.astype(F32) + part).astype(BF), payload)
            carried[way] = along(payload, way)
        for way in (1, -1):
            if step < LINE - 1:
                position = place if way == 1 else LINE - 1 - place
                source = position - 1 - step
                valid = source >= 0
                source = jnp.clip(source, 0, LINE - 1)
                source = source if way == 1 else LINE - 1 - source
                features = jnp.where(valid, up_block(source), jnp.zeros((), BF))
                hg_total = hg_total + contract(features, carried[way], ((1,), (1,)))

    own_part = lax.optimization_barrier(contract(hidden_t, own_up, ((1,), (0,))))
    grads = (own_part + carried[1].astype(F32) + carried[-1].astype(F32)) * scale_hid

    count = (step_index[0] + 1).astype(F32)
    first_new = 0.9 * first_moment + 0.1 * grads
    second_new = 0.999 * second_moment + 0.001 * grads * grads
    correct_one = 1.0 - jnp.power(F32(0.9), count)
    correct_two = 1.0 - jnp.power(F32(0.999), count)
    weights_f = weights.astype(F32)
    step_size = first_new / correct_one / (jnp.sqrt(second_new / correct_two) + 1e-08) + 0.1 * weights_f
    updated = (weights_f - 0.05 * step_size).astype(BF)

    half = updated.shape[0] // 2
    even_step = step_index[0] % 2 == 0
    lower, upper = updated[:half], updated[half:]
    near = lax.ppermute(jnp.where(even_step, lower, upper), "y", [(i, (i + 1) % 4) for i in range(4)])
    far = lax.ppermute(jnp.where(even_step, upper, lower), "y", [(i, (i + 2) % 4) for i in range(4)])
    partner = jnp.concatenate([jnp.where(even_step, near, far), jnp.where(even_step, far, near)], 0)
    mixed = ((updated.astype(F32) + partner.astype(F32)) * 0.5).astype(BF)

    in_grad = (hg_total * scale_hid).astype(BF)
    return mixed, first_new, second_new, in_grad


def solution(mesh):
    split = Mesh(mesh.devices.reshape(4, LINE, 2, 4, 2), ("y", "zl", "zh", "x", "c"))
    rep, tp = ("y", "zl"), ("zh", "x", "c")
    in_specs = (P(rep, tp), P(rep, tp), P(tp, rep), P(tp, rep), P(tp, rep), P())
    out_specs = (P(tp, rep), P(tp, rep), P(tp, rep), P(rep, tp))
    return jax.shard_map(body, mesh=split, in_specs=in_specs, out_specs=out_specs, check_vma=False)
```

```python
import math

import jax
import jax.numpy as jnp
from jax import lax
from jax.sharding import Mesh, PartitionSpec as P

BF = jnp.bfloat16
F32 = jnp.float32
LINE = 8


def along(value, way, step):
    chips = range(step + 1) if way == 1 else range(LINE - 1, LINE - 2 - step, -1)
    return lax.ppermute(value, "zl", [(chip, chip + way) for chip in chips])


def contract(left, right, dims):
    return lax.dot_general(left, right, (dims, ((), ())), preferred_element_type=F32)


def body(hidden, upstream, weights, first_moment, second_moment, step_index):
    width = weights.shape[1]
    place, far_half = lax.axis_index("zl"), lax.axis_index("zh")
    scale_hid = 1.0 / math.sqrt(7168)
    never = step_index[0] < 0

    all_weights = lax.all_gather(weights, "zl", axis=1, tiled=True)
    up_other = lax.ppermute(upstream, "zh", [(0, 1), (1, 0)])
    near_up = lax.all_gather(upstream, ("x", "c"), axis=1, tiled=True)
    far_up = lax.all_gather(up_other, ("x", "c"), axis=1, tiled=True)
    full_up = jnp.concatenate([near_up, far_up], axis=1)
    hidden_t = lax.optimization_barrier(hidden.T)

    def up_block(index):
        at = jnp.bitwise_xor(index, 4 * far_half) * width
        return lax.dynamic_slice_in_dim(full_up, at, width, 1)

    carried, sent = {}, {}
    for step in range(LINE - 1):
        for way in (1, -1):
            position = place if way == 1 else LINE - 1 - place
            block = jnp.clip(LINE - 1 - step + position, 0, LINE - 1)
            block = block if way == 1 else LINE - 1 - block
            features = up_block(block)
            if step > 0:
                features = jnp.where(never, sent[way], features)
            part = lax.optimization_barrier(contract(hidden_t, features, ((1,), (0,))))
            sent[way] = (part + carried[way].astype(F32) if step > 0 else part).astype(BF)
            carried[way] = along(sent[way], way, step)

    own_up = jnp.where(never, sent[1], up_block(place))
    own_part = lax.optimization_barrier(contract(hidden_t, own_up, ((1,), (0,))))
    grads = (own_part + carried[1].astype(F32) + carried[-1].astype(F32)) * scale_hid

    count = (step_index[0] + 1).astype(F32)
    first_new = 0.9 * first_moment + 0.1 * grads
    second_new = 0.999 * second_moment + 0.001 * grads * grads
    correct_one = 1.0 - jnp.power(F32(0.9), count)
    correct_two = 1.0 - jnp.power(F32(0.999), count)
    weights_f = weights.astype(F32)
    step_size = first_new / correct_one / (jnp.sqrt(second_new / correct_two) + 1e-08) + 0.1 * weights_f
    updated = (weights_f - 0.05 * step_size).astype(BF)

    half = updated.shape[0] // 2
    even_step = step_index[0] % 2 == 0
    lower, upper = updated[:half], updated[half:]
    near = lax.ppermute(jnp.where(even_step, lower, upper), "y", [(i, (i + 1) % 4) for i in range(4)])
    far = lax.ppermute(jnp.where(even_step, upper, lower), "y", [(i, (i + 2) % 4) for i in range(4)])
    partner = jnp.concatenate([jnp.where(even_step, near, far), jnp.where(even_step, far, near)], 0)
    mixed = ((updated.astype(F32) + partner.astype(F32)) * 0.5).astype(BF)

    ordered_up = jnp.where(far_half == 0, full_up, jnp.concatenate([far_up, near_up], axis=1))
    in_grad = (contract(ordered_up, all_weights, ((1,), (1,))) * scale_hid).astype(BF)
    return mixed, first_new, second_new, in_grad


def solution(mesh):
    split = Mesh(mesh.devices.reshape(4, LINE, 2, 4, 2), ("y", "zl", "zh", "x", "c"))
    rep, tp = ("y", "zl"), ("zh", "x", "c")
    in_specs = (P(rep, tp), P(rep, tp), P(tp, rep), P(tp, rep), P(tp, rep), P())
    out_specs = (P(tp, rep), P(tp, rep), P(tp, rep), P(rep, tp))
    return jax.shard_map(body, mesh=split, in_specs=in_specs, out_specs=out_specs, check_vma=False)
```

```python
import math

import jax
import jax.numpy as jnp
from jax import lax
from jax.sharding import Mesh, PartitionSpec as P

BF = jnp.bfloat16
F32 = jnp.float32
LINE = 8
LEAD = 1


def along(value, way):
    return lax.ppermute(value, "zl", [(i, i + way) for i in range(LINE) if 0 <= i + way < LINE])


def contract(left, right, dims):
    return lax.dot_general(left, right, (dims, ((), ())), preferred_element_type=F32)


def body(hidden, upstream, weights, first_moment, second_moment, step_index):
    width = weights.shape[1]
    place, far_half = lax.axis_index("zl"), lax.axis_index("zh")
    scale_hid = 1.0 / math.sqrt(7168)

    def behind(value, other):
        return jnp.where(step_index[0] < 0, other, value)

    up_other = lax.ppermute(upstream, "zh", [(0, 1), (1, 0)])
    near_up = lax.all_gather(upstream, ("x", "c"), axis=1, tiled=True)
    far_up = lax.all_gather(up_other, ("x", "c"), axis=1, tiled=True)
    full_up = jnp.concatenate([near_up, far_up], axis=1)
    hidden_t = lax.optimization_barrier(hidden.T)

    def up_block(index):
        at = jnp.bitwise_xor(index, 4 * far_half) * width
        return lax.dynamic_slice_in_dim(full_up, at, width, 1)

    start = behind(weights, near_up[:, :width])
    carried, sent = {1: start, -1: start}, {}
    hg_total = contract(behind(up_block(place), start), weights, ((1,), (1,)))
    for step in range(LINE - 1 + LEAD):
        turn = step - LEAD
        for way in (1, -1):
            position = place if way == 1 else LINE - 1 - place
            payload = carried[way]
            if turn >= 0:
                block = jnp.clip(LINE - 1 - turn + position, 0, LINE - 1)
                block = block if way == 1 else LINE - 1 - block
                features = up_block(block)
                if turn > 0:
                    features = behind(features, sent[way])
                part = lax.optimization_barrier(contract(hidden_t, features, ((1,), (0,))))
                payload = jnp.where(position <= turn, (payload.astype(F32) + part).astype(BF), payload)
            sent[way] = payload
            carried[way] = along(payload, way)
        for way in (1, -1):
            if step < LINE - 1:
                position = place if way == 1 else LINE - 1 - place
                source = position - 1 - step
                valid = source >= 0
                source = jnp.clip(source, 0, LINE - 1)
                source = source if way == 1 else LINE - 1 - source
                features = jnp.where(valid, up_block(source), jnp.zeros((), BF))
                hg_total = hg_total + contract(features, carried[way], ((1,), (1,)))

    own_up = behind(up_block(place), sent[1])
    own_part = lax.optimization_barrier(contract(hidden_t, own_up, ((1,), (0,))))
    grads = (own_part + carried[1].astype(F32) + carried[-1].astype(F32)) * scale_hid

    count = (step_index[0] + 1).astype(F32)
    first_new = 0.9 * first_moment + 0.1 * grads
    second_new = 0.999 * second_moment + 0.001 * grads * grads
    correct_one = 1.0 - jnp.power(F32(0.9), count)
    correct_two = 1.0 - jnp.power(F32(0.999), count)
    weights_f = weights.astype(F32)
    step_size = first_new / correct_one / (jnp.sqrt(second_new / correct_two) + 1e-08) + 0.1 * weights_f
    updated = (weights_f - 0.05 * step_size).astype(BF)

    half = updated.shape[0] // 2
    even_step = step_index[0] % 2 == 0
    lower, upper = updated[:half], updated[half:]
    near = lax.ppermute(jnp.where(even_step, lower, upper), "y", [(i, (i + 1) % 4) for i in range(4)])
    far = lax.ppermute(jnp.where(even_step, upper, lower), "y", [(i, (i + 2) % 4) for i in range(4)])
    partner = jnp.concatenate([jnp.where(even_step, near, far), jnp.where(even_step, far, near)], 0)
    mixed = ((updated.astype(F32) + partner.astype(F32)) * 0.5).astype(BF)

    in_grad = (hg_total * scale_hid).astype(BF)
    return mixed, first_new, second_new, in_grad


def solution(mesh):
    split = Mesh(mesh.devices.reshape(4, LINE, 2, 4, 2), ("y", "zl", "zh", "x", "c"))
    rep, tp = ("y", "zl"), ("zh", "x", "c")
    in_specs = (P(rep, tp), P(rep, tp), P(tp, rep), P(tp, rep), P(tp, rep), P())
    out_specs = (P(tp, rep), P(tp, rep), P(tp, rep), P(rep, tp))
    return jax.shard_map(body, mesh=split, in_specs=in_specs, out_specs=out_specs, check_vma=False)
```

```python
import math

import jax
import jax.numpy as jnp
from jax import lax
from jax.sharding import Mesh, PartitionSpec as P

BF = jnp.bfloat16
F32 = jnp.float32
LINE = 8


def along(value, early):
    pairs = []
    for half in range(2):
        way = 1 if (half == 1) == early else -1
        pairs += [(i * 2 + half, (i + way) * 2 + half) for i in range(LINE) if 0 <= i + way < LINE]
    return lax.ppermute(value, ("zl", "zh"), pairs)


def contract(left, right, dims):
    return lax.dot_general(left, right, (dims, ((), ())), preferred_element_type=F32)


def body(hidden, upstream, weights, first_moment, second_moment, step_index):
    width = weights.shape[1]
    place, far_half = lax.axis_index("zl"), lax.axis_index("zh")
    scale_hid = 1.0 / math.sqrt(7168)

    def behind(value, other):
        return jnp.where(step_index[0] < 0, other, value)

    last = LINE - 1
    early_up = far_half == 1
    position = jnp.where(early_up, place, last - place)

    up_other = lax.ppermute(upstream, "zh", [(0, 1), (1, 0)])
    hidden_t = lax.optimization_barrier(hidden.T)
    got = {True: [along(weights, True)], False: []}
    sent = {}

    def send(early, turn, part):
        here = position if early else last - position
        arrived = got[early][-1]
        total = (arrived.astype(F32) + part).astype(BF)
        sent[early, turn] = jnp.where(here <= turn, total, arrived)
        got[early].append(along(sent[early, turn], early))

    def product(features):
        return lax.optimization_barrier(contract(hidden_t, features, ((1,), (0,))))

    near_up = lax.all_gather(upstream, ("x", "c"), axis=1, tiled=True)
    got[False].append(along(behind(weights, near_up[:, :width]), False))
    first = lax.dynamic_slice_in_dim(near_up, jnp.where(early_up, 3, 0) * width, width, 1)
    send(True, 0, product(first))
    up_other = behind(up_other, sent[True, 0][:, : up_other.shape[1]])
    far_up = lax.all_gather(up_other, ("x", "c"), axis=1, tiled=True)
    full_up = jnp.concatenate([near_up, far_up], axis=1)

    def up_block(index):
        at = jnp.bitwise_xor(index, 4 * far_half) * width
        return lax.dynamic_slice_in_dim(full_up, at, width, 1)

    def features_of(pair):
        index = jnp.where(pair >= position, last - pair + position, position - 1 - pair)
        return up_block(jnp.where(early_up, index, last - index))

    parts = {}

    def part_of(pair, after):
        if pair not in parts:
            features = features_of(pair)
            parts[pair] = product(features if after is None else behind(features, sent[after]))
        return parts[pair]

    hg_total = contract(behind(up_block(place), sent[True, 0]), weights, ((1,), (1,)))
    for turn in range(last):
        send(False, turn, part_of(last - 1 - turn, (False, turn - 1) if 0 < turn < last - 1 else (False, 3) if turn else None))
        if turn < last - 1:
            send(True, turn + 1, part_of(turn + 1, (True, turn) if turn else None))
        for pair in {turn, last - 1 - turn} if turn >= last // 2 else ():
            block = jnp.where(pair < position, got[True][pair], got[False][last - 1 - pair])
            hg_total = hg_total + contract(features_of(pair), block, ((1,), (1,)))

    own_part = product(behind(up_block(place), sent[False, 4]))
    grads = (own_part + got[True][-1].astype(F32) + got[False][-1].astype(F32)) * scale_hid

    count = (step_index[0] + 1).astype(F32)
    first_new = 0.9 * first_moment + 0.1 * grads
    second_new = 0.999 * second_moment + 0.001 * grads * grads
    correct_one = 1.0 - jnp.power(F32(0.9), count)
    correct_two = 1.0 - jnp.power(F32(0.999), count)
    weights_f = weights.astype(F32)
    step_size = first_new / correct_one / (jnp.sqrt(second_new / correct_two) + 1e-08) + 0.1 * weights_f
    updated = (weights_f - 0.05 * step_size).astype(BF)

    half = updated.shape[0] // 2
    even_step = step_index[0] % 2 == 0
    lower, upper = updated[:half], updated[half:]
    near = lax.ppermute(jnp.where(even_step, lower, upper), "y", [(i, (i + 1) % 4) for i in range(4)])
    far = lax.ppermute(jnp.where(even_step, upper, lower), "y", [(i, (i + 2) % 4) for i in range(4)])
    partner = jnp.concatenate([jnp.where(even_step, near, far), jnp.where(even_step, far, near)], 0)
    mixed = ((updated.astype(F32) + partner.astype(F32)) * 0.5).astype(BF)

    in_grad = (hg_total * scale_hid).astype(BF)
    return mixed, first_new, second_new, in_grad


def solution(mesh):
    split = Mesh(mesh.devices.reshape(4, LINE, 2, 4, 2), ("y", "zl", "zh", "x", "c"))
    rep, tp = ("y", "zl"), ("zh", "x", "c")
    in_specs = (P(rep, tp), P(rep, tp), P(tp, rep), P(tp, rep), P(tp, rep), P())
    out_specs = (P(tp, rep), P(tp, rep), P(tp, rep), P(rep, tp))
    return jax.shard_map(body, mesh=split, in_specs=in_specs, out_specs=out_specs, check_vma=False)
```

```python
import math

import jax
import jax.numpy as jnp
from jax import lax
from jax.sharding import Mesh, PartitionSpec as P

BF = jnp.bfloat16
F32 = jnp.float32
LINE = 8


def along(value, early):
    pairs = []
    for half in range(2):
        way = 1 if (half == 1) == early else -1
        pairs += [(i * 2 + half, (i + way) * 2 + half) for i in range(LINE) if 0 <= i + way < LINE]
    return lax.ppermute(value, ("zl", "zh"), pairs)


def contract(left, right, dims):
    return lax.dot_general(left, right, (dims, ((), ())), preferred_element_type=F32)


def body(hidden, upstream, weights, first_moment, second_moment, step_index):
    width = weights.shape[1]
    place, far_half = lax.axis_index("zl"), lax.axis_index("zh")
    scale_hid = 1.0 / math.sqrt(7168)

    def behind(value, other):
        return jnp.where(step_index[0] < 0, other, value)

    last = LINE - 1
    early_up = far_half == 1
    position = jnp.where(early_up, place, last - place)

    up_other = lax.ppermute(upstream, "zh", [(0, 1), (1, 0)])
    hidden_t = lax.optimization_barrier(hidden.T)
    got = {True: [along(weights, True)], False: []}
    sent = {}

    def send(early, turn, part):
        here = position if early else last - position
        arrived = got[early][-1]
        if sent:
            arrived = behind(arrived, list(sent.values())[-1])
        total = (arrived.astype(F32) + part).astype(BF)
        sent[early, turn] = lax.optimization_barrier(jnp.where(here <= turn, total, arrived))
        got[early].append(along(sent[early, turn], early))

    def product(features):
        return lax.optimization_barrier(contract(hidden_t, features, ((1,), (0,))))

    near_up = lax.all_gather(upstream, ("x", "c"), axis=1, tiled=True)
    got[False].append(along(behind(weights, near_up[:, :width]), False))
    first = lax.dynamic_slice_in_dim(near_up, jnp.where(early_up, 3, 0) * width, width, 1)
    send(True, 0, product(first))
    up_other = behind(up_other, sent[True, 0][:, : up_other.shape[1]])
    far_up = lax.all_gather(up_other, ("x", "c"), axis=1, tiled=True)
    full_up = jnp.concatenate([near_up, far_up], axis=1)

    def up_block(index):
        at = jnp.bitwise_xor(index, 4 * far_half) * width
        return lax.dynamic_slice_in_dim(full_up, at, width, 1)

    def features_of(pair):
        index = jnp.where(pair >= position, last - pair + position, position - 1 - pair)
        return up_block(jnp.where(early_up, index, last - index))

    parts = {}

    def part_of(pair, after):
        if pair not in parts:
            features = features_of(pair)
            parts[pair] = product(features if after is None else behind(features, sent[after]))
        return parts[pair]

    hg_total = contract(behind(up_block(place), sent[True, 0]), weights, ((1,), (1,)))
    for turn in range(last):
        send(False, turn, part_of(last - 1 - turn, (False, turn - 1) if 0 < turn < last - 1 else (False, 3) if turn else None))
        if turn < last - 1:
            send(True, turn + 1, part_of(turn + 1, (True, turn) if turn else None))
        for pair in {turn, last - 1 - turn} if turn >= last // 2 else ():
            block = jnp.where(pair < position, got[True][pair], got[False][last - 1 - pair])
            hg_total = hg_total + contract(features_of(pair), block, ((1,), (1,)))

    own_part = product(behind(up_block(place), sent[False, 4]))
    grads = (own_part + got[True][-1].astype(F32) + got[False][-1].astype(F32)) * scale_hid

    count = (step_index[0] + 1).astype(F32)
    first_new = 0.9 * first_moment + 0.1 * grads
    second_new = 0.999 * second_moment + 0.001 * grads * grads
    correct_one = 1.0 - jnp.power(F32(0.9), count)
    correct_two = 1.0 - jnp.power(F32(0.999), count)
    weights_f = weights.astype(F32)
    step_size = first_new / correct_one / (jnp.sqrt(second_new / correct_two) + 1e-08) + 0.1 * weights_f
    updated = (weights_f - 0.05 * step_size).astype(BF)

    half = updated.shape[0] // 2
    even_step = step_index[0] % 2 == 0
    lower, upper = updated[:half], updated[half:]
    near = lax.ppermute(jnp.where(even_step, lower, upper), "y", [(i, (i + 1) % 4) for i in range(4)])
    far = lax.ppermute(jnp.where(even_step, upper, lower), "y", [(i, (i + 2) % 4) for i in range(4)])
    partner = jnp.concatenate([jnp.where(even_step, near, far), jnp.where(even_step, far, near)], 0)
    mixed = ((updated.astype(F32) + partner.astype(F32)) * 0.5).astype(BF)

    in_grad = (hg_total * scale_hid).astype(BF)
    return mixed, first_new, second_new, in_grad


def solution(mesh):
    split = Mesh(mesh.devices.reshape(4, LINE, 2, 4, 2), ("y", "zl", "zh", "x", "c"))
    rep, tp = ("y", "zl"), ("zh", "x", "c")
    in_specs = (P(rep, tp), P(rep, tp), P(tp, rep), P(tp, rep), P(tp, rep), P())
    out_specs = (P(tp, rep), P(tp, rep), P(tp, rep), P(rep, tp))
    return jax.shard_map(body, mesh=split, in_specs=in_specs, out_specs=out_specs, check_vma=False)
```

```python
import math

import jax
import jax.numpy as jnp
from jax import lax
from jax.sharding import Mesh, PartitionSpec as P

BF = jnp.bfloat16
F32 = jnp.float32
LINE = 8


def along(value, way):
    return lax.ppermute(value, "zl", [(i, i + way) for i in range(LINE) if 0 <= i + way < LINE])


def contract(left, right, dims):
    return lax.dot_general(left, right, (dims, ((), ())), preferred_element_type=F32)


def body(hidden, upstream, weights, first_moment, second_moment, step_index):
    width = weights.shape[1]
    place, far_half = lax.axis_index("zl"), lax.axis_index("zh")
    scale_hid = 1.0 / math.sqrt(7168)

    def behind(value, other):
        return jnp.where(step_index[0] < 0, other, value)

    last = LINE - 1
    piece = width // 2
    second_core = lax.axis_index("c") == 1

    up_other = lax.ppermute(upstream, "zh", [(0, 1), (1, 0)])
    hidden_t = lax.optimization_barrier(hidden.T)
    got = {True: [along(weights, 1)], False: [along(weights, -1)]}
    sent = {}

    for hop in (got[True][0], got[False][0]):
        up_other = behind(up_other, hop[:, : up_other.shape[1]])
    of_core = lax.all_gather(jnp.concatenate([upstream, up_other], 1), "x", axis=1, tiled=True)
    of_other = lax.ppermute(of_core, "c", [(0, 1), (1, 0)])
    of_first = jnp.where(second_core, of_other, of_core)
    of_second = jnp.where(second_core, of_core, of_other)
    cuts = range(0, of_core.shape[1], piece)
    full_up = jnp.concatenate([part[:, at : at + piece] for at in cuts for part in (of_first, of_second)], 1)
    full_up = lax.optimization_barrier(full_up)

    def up_block(index):
        at = 2 * jnp.bitwise_and(index, 3) + jnp.bitwise_xor(index // 4, far_half)
        return lax.dynamic_slice_in_dim(full_up, at * width, width, 1)

    def send(up, turn, part):
        arrived = got[up][-1]
        if sent:
            arrived = behind(arrived, list(sent.values())[-1])
        total = (arrived.astype(F32) + part).astype(BF)
        ready = (place if up else last - place) <= turn
        sent[up, turn] = lax.optimization_barrier(jnp.where(ready, total, arrived))
        got[up].append(along(sent[up, turn], 1 if up else -1))

    def product(features):
        return lax.optimization_barrier(contract(hidden_t, features, ((1,), (0,))))

    def features_of(pair):
        return up_block(jnp.where(pair >= place, last - pair + place, place - 1 - pair))

    parts = {}

    def part_of(pair, after):
        if pair not in parts:
            features = features_of(pair)
            parts[pair] = product(behind(features, sent[after]) if after in sent else features)
        return parts[pair]

    hg_total = 0.0
    for turn in range(last):
        send(True, turn, part_of(turn, (True, turn - 1)))
        send(False, turn, part_of(last - 1 - turn, (False, turn - 1)))
        for pair in sorted({turn, last - 1 - turn}) if turn >= last // 2 else ():
            block = jnp.where(pair < place, got[True][pair], got[False][last - 1 - pair])
            hg_total = hg_total + contract(features_of(pair), block, ((1,), (1,)))

    own_up = behind(up_block(place), sent[True, 4])
    hg_total = hg_total + contract(own_up, weights, ((1,), (1,)))
    own_part = product(own_up)
    grads = (own_part + got[True][-1].astype(F32) + got[False][-1].astype(F32)) * scale_hid

    count = (step_index[0] + 1).astype(F32)
    first_new = 0.9 * first_moment + 0.1 * grads
    second_new = 0.999 * second_moment + 0.001 * grads * grads
    correct_one = 1.0 - jnp.power(F32(0.9), count)
    correct_two = 1.0 - jnp.power(F32(0.999), count)
    weights_f = weights.astype(F32)
    step_size = first_new / correct_one / (jnp.sqrt(second_new / correct_two) + 1e-08) + 0.1 * weights_f
    updated = (weights_f - 0.05 * step_size).astype(BF)

    half = updated.shape[0] // 2
    even_step = step_index[0] % 2 == 0
    lower, upper = updated[:half], updated[half:]
    near = lax.ppermute(jnp.where(even_step, lower, upper), "y", [(i, (i + 1) % 4) for i in range(4)])
    far = lax.ppermute(jnp.where(even_step, upper, lower), "y", [(i, (i + 2) % 4) for i in range(4)])
    partner = jnp.concatenate([jnp.where(even_step, near, far), jnp.where(even_step, far, near)], 0)
    mixed = ((updated.astype(F32) + partner.astype(F32)) * 0.5).astype(BF)

    in_grad = (hg_total * scale_hid).astype(BF)
    return mixed, first_new, second_new, in_grad


def solution(mesh):
    split = Mesh(mesh.devices.reshape(4, LINE, 2, 4, 2), ("y", "zl", "zh", "x", "c"))
    rep, tp = ("y", "zl"), ("zh", "x", "c")
    in_specs = (P(rep, tp), P(rep, tp), P(tp, rep), P(tp, rep), P(tp, rep), P())
    out_specs = (P(tp, rep), P(tp, rep), P(tp, rep), P(rep, tp))
    return jax.shard_map(body, mesh=split, in_specs=in_specs, out_specs=out_specs, check_vma=False)
```

```python
import math

import jax
import jax.numpy as jnp
from jax import lax
from jax.sharding import Mesh, PartitionSpec as P

BF = jnp.bfloat16
F32 = jnp.float32
LINE = 8


def along(value, way):
    return lax.ppermute(value, "zl", [(i, i + way) for i in range(LINE) if 0 <= i + way < LINE])


def contract(left, right, dims):
    return lax.dot_general(left, right, (dims, ((), ())), preferred_element_type=F32)


def body(hidden, upstream, weights, first_moment, second_moment, step_index):
    width = weights.shape[1]
    place, far_half = lax.axis_index("zl"), lax.axis_index("zh")
    scale_hid = 1.0 / math.sqrt(7168)

    def behind(value, other):
        return jnp.where(step_index[0] < 0, other, value)

    last = LINE - 1
    piece = width // 2
    second_core = lax.axis_index("c") == 1

    up_other = lax.ppermute(upstream, "zh", [(0, 1), (1, 0)])
    hidden_t = lax.optimization_barrier(hidden.T)
    both_up = lax.optimization_barrier(jnp.concatenate([upstream, up_other], 1))
    weights_after = lax.optimization_barrier(behind(weights, both_up))
    got = {True: [along(weights_after, 1)], False: [along(weights_after, -1)]}
    sent = {}

    of_core = lax.all_gather(behind(both_up, weights_after), "x", axis=1, tiled=True)
    to_other = of_core
    for hop in (got[True][0], got[False][0]):
        to_other = behind(to_other, jnp.concatenate([hop] * (of_core.shape[1] // width), 1))
    of_other = lax.ppermute(to_other, "c", [(0, 1), (1, 0)])
    of_first = jnp.where(second_core, of_other, of_core)
    of_second = jnp.where(second_core, of_core, of_other)
    cuts = range(0, of_core.shape[1], piece)
    full_up = jnp.concatenate([part[:, at : at + piece] for at in cuts for part in (of_first, of_second)], 1)
    full_up = lax.optimization_barrier(full_up)

    def up_block(index):
        at = 2 * jnp.bitwise_and(index, 3) + jnp.bitwise_xor(index // 4, far_half)
        return lax.dynamic_slice_in_dim(full_up, at * width, width, 1)

    def send(up, turn, part):
        arrived = got[up][-1]
        if sent:
            arrived = behind(arrived, list(sent.values())[-1])
        total = (arrived.astype(F32) + part).astype(BF)
        ready = (place if up else last - place) <= turn
        sent[up, turn] = lax.optimization_barrier(jnp.where(ready, total, arrived))
        got[up].append(along(sent[up, turn], 1 if up else -1))

    def product(features):
        return lax.optimization_barrier(contract(hidden_t, features, ((1,), (0,))))

    def features_of(pair):
        return up_block(jnp.where(pair >= place, last - pair + place, place - 1 - pair))

    parts = {}

    def part_of(pair, after):
        if pair not in parts:
            features = features_of(pair)
            parts[pair] = product(behind(features, sent[after]) if after in sent else features)
        return parts[pair]

    hg_total = 0.0
    for turn in range(last):
        send(True, turn, part_of(turn, (True, turn - 1)))
        send(False, turn, part_of(last - 1 - turn, (False, turn - 1)))
        for pair in sorted({turn, last - 1 - turn}) if turn >= last // 2 else ():
            block = jnp.where(pair < place, got[True][pair], got[False][last - 1 - pair])
            hg_total = hg_total + contract(features_of(pair), block, ((1,), (1,)))

    own_up = behind(up_block(place), sent[True, 4])
    hg_total = hg_total + contract(own_up, weights, ((1,), (1,)))
    own_part = product(own_up)
    grads = (own_part + got[True][-1].astype(F32) + got[False][-1].astype(F32)) * scale_hid

    count = (step_index[0] + 1).astype(F32)
    first_new = 0.9 * first_moment + 0.1 * grads
    second_new = 0.999 * second_moment + 0.001 * grads * grads
    correct_one = 1.0 - jnp.power(F32(0.9), count)
    correct_two = 1.0 - jnp.power(F32(0.999), count)
    weights_f = weights.astype(F32)
    step_size = first_new / correct_one / (jnp.sqrt(second_new / correct_two) + 1e-08) + 0.1 * weights_f
    updated = (weights_f - 0.05 * step_size).astype(BF)

    half = updated.shape[0] // 2
    even_step = step_index[0] % 2 == 0
    lower, upper = updated[:half], updated[half:]
    far = lax.ppermute(jnp.where(even_step, upper, lower), "y", [(i, (i + 2) % 4) for i in range(4)])
    near = lax.ppermute(jnp.where(even_step, lower, upper), "y", [(i, (i + 1) % 4) for i in range(4)])
    partner = jnp.concatenate([jnp.where(even_step, near, far), jnp.where(even_step, far, near)], 0)
    mixed = ((updated.astype(F32) + partner.astype(F32)) * 0.5).astype(BF)

    in_grad = (hg_total * scale_hid).astype(BF)
    return mixed, first_new, second_new, in_grad


def solution(mesh):
    split = Mesh(mesh.devices.reshape(4, LINE, 2, 4, 2), ("y", "zl", "zh", "x", "c"))
    rep, tp = ("y", "zl"), ("zh", "x", "c")
    in_specs = (P(rep, tp), P(rep, tp), P(tp, rep), P(tp, rep), P(tp, rep), P())
    out_specs = (P(tp, rep), P(tp, rep), P(tp, rep), P(rep, tp))
    return jax.shard_map(body, mesh=split, in_specs=in_specs, out_specs=out_specs, check_vma=False)
```

```python
import math

import jax
import jax.numpy as jnp
from jax import lax
from jax.sharding import Mesh, PartitionSpec as P

BF = jnp.bfloat16
F32 = jnp.float32
LINE = 8


def along(value, early):
    pairs = []
    for half in range(2):
        way = 1 if (half == 1) == early else -1
        pairs += [(i * 2 + half, (i + way) * 2 + half) for i in range(LINE) if 0 <= i + way < LINE]
    return lax.ppermute(value, ("zl", "zh"), pairs)


def contract(left, right, dims):
    return lax.dot_general(left, right, (dims, ((), ())), preferred_element_type=F32)


def body(hidden, upstream, weights, first_moment, second_moment, step_index):
    width = weights.shape[1]
    place, far_half = lax.axis_index("zl"), lax.axis_index("zh")
    scale_hid = 1.0 / math.sqrt(7168)

    def behind(value, other):
        return jnp.where(step_index[0] < 0, other, value)

    last = LINE - 1
    early_up = far_half == 1
    position = jnp.where(early_up, place, last - place)

    up_other = lax.ppermute(upstream, "zh", [(0, 1), (1, 0)])
    hidden_t = lax.optimization_barrier(hidden.T)
    got = {True: [along(weights, True)], False: [along(weights, False)]}
    sent = {}

    def send(early, turn, part):
        here = position if early else last - position
        arrived = got[early][-1]
        arrived = behind(arrived, list(sent.values())[-1] if sent else got[not early][-1])
        total = (arrived.astype(F32) + part).astype(BF)
        sent[early, turn] = lax.optimization_barrier(jnp.where(here <= turn, total, arrived))
        got[early].append(along(sent[early, turn], early))

    def product(features):
        return lax.optimization_barrier(contract(hidden_t, features, ((1,), (0,))))

    near_up = lax.all_gather(upstream, ("x", "c"), axis=1, tiled=True)
    first = lax.dynamic_slice_in_dim(near_up, jnp.where(early_up, 3, 0) * width, width, 1)
    send(True, 0, product(first))
    up_other = behind(up_other, sent[True, 0][:, : up_other.shape[1]])
    far_up = lax.all_gather(up_other, ("x", "c"), axis=1, tiled=True)
    full_up = jnp.concatenate([near_up, far_up], axis=1)

    def up_block(index):
        at = jnp.bitwise_xor(index, 4 * far_half) * width
        return lax.dynamic_slice_in_dim(full_up, at, width, 1)

    def features_of(pair):
        index = jnp.where(pair >= position, last - pair + position, position - 1 - pair)
        return up_block(jnp.where(early_up, index, last - index))

    parts = {}

    def part_of(pair, after):
        if pair not in parts:
            features = features_of(pair)
            parts[pair] = product(features if after is None else behind(features, sent[after]))
        return parts[pair]

    hg_total = contract(behind(up_block(place), sent[True, 0]), weights, ((1,), (1,)))
    for turn in range(last):
        send(False, turn, part_of(last - 1 - turn, (False, turn - 1) if 0 < turn < last - 1 else (False, 3) if turn else None))
        if turn < last - 1:
            send(True, turn + 1, part_of(turn + 1, (True, turn) if turn else None))
        for pair in {turn, last - 1 - turn} if turn >= last // 2 else ():
            block = jnp.where(pair < position, got[True][pair], got[False][last - 1 - pair])
            hg_total = hg_total + contract(features_of(pair), block, ((1,), (1,)))

    own_part = product(behind(up_block(place), sent[False, 4]))
    grads = (own_part + got[True][-1].astype(F32) + got[False][-1].astype(F32)) * scale_hid

    count = (step_index[0] + 1).astype(F32)
    first_new = 0.9 * first_moment + 0.1 * grads
    second_new = 0.999 * second_moment + 0.001 * grads * grads
    correct_one = 1.0 - jnp.power(F32(0.9), count)
    correct_two = 1.0 - jnp.power(F32(0.999), count)
    weights_f = weights.astype(F32)
    step_size = first_new / correct_one / (jnp.sqrt(second_new / correct_two) + 1e-08) + 0.1 * weights_f
    updated = (weights_f - 0.05 * step_size).astype(BF)

    half = updated.shape[0] // 2
    even_step = step_index[0] % 2 == 0
    lower, upper = updated[:half], updated[half:]
    near = lax.ppermute(jnp.where(even_step, lower, upper), "y", [(i, (i + 1) % 4) for i in range(4)])
    far = lax.ppermute(jnp.where(even_step, upper, lower), "y", [(i, (i + 2) % 4) for i in range(4)])
    partner = jnp.concatenate([jnp.where(even_step, near, far), jnp.where(even_step, far, near)], 0)
    mixed = ((updated.astype(F32) + partner.astype(F32)) * 0.5).astype(BF)

    in_grad = (hg_total * scale_hid).astype(BF)
    return mixed, first_new, second_new, in_grad


def solution(mesh):
    split = Mesh(mesh.devices.reshape(4, LINE, 2, 4, 2), ("y", "zl", "zh", "x", "c"))
    rep, tp = ("y", "zl"), ("zh", "x", "c")
    in_specs = (P(rep, tp), P(rep, tp), P(tp, rep), P(tp, rep), P(tp, rep), P())
    out_specs = (P(tp, rep), P(tp, rep), P(tp, rep), P(rep, tp))
    return jax.shard_map(body, mesh=split, in_specs=in_specs, out_specs=out_specs, check_vma=False)
```

```python
import math

import jax
import jax.numpy as jnp
from jax import lax
from jax.sharding import Mesh, PartitionSpec as P

BF = jnp.bfloat16
F32 = jnp.float32
LINE = 8


def along(value, early):
    pairs = []
    for half in range(2):
        way = 1 if (half == 1) == early else -1
        pairs += [(i * 2 + half, (i + way) * 2 + half) for i in range(LINE) if 0 <= i + way < LINE]
    return lax.ppermute(value, ("zl", "zh"), pairs)


def contract(left, right, dims):
    return lax.dot_general(left, right, (dims, ((), ())), preferred_element_type=F32)


def body(hidden, upstream, weights, first_moment, second_moment, step_index):
    width = weights.shape[1]
    place, far_half = lax.axis_index("zl"), lax.axis_index("zh")
    scale_hid = 1.0 / math.sqrt(7168)

    def behind(value, other):
        return jnp.where(step_index[0] < 0, other, value)

    last = LINE - 1
    early_up = far_half == 1
    position = jnp.where(early_up, place, last - place)

    hidden_t = lax.optimization_barrier(hidden.T)
    got = {True: [along(weights, True)], False: [along(weights, False)]}
    up_other = lax.ppermute(upstream, "zh", [(0, 1), (1, 0)])
    sent = {}

    def send(early, turn, part):
        here = position if early else last - position
        arrived = got[early][-1]
        arrived = behind(arrived, list(sent.values())[-1] if sent else got[not early][-1])
        total = (arrived.astype(F32) + part).astype(BF)
        sent[early, turn] = lax.optimization_barrier(jnp.where(here <= turn, total, arrived))
        got[early].append(along(sent[early, turn], early))

    def product(features):
        return lax.optimization_barrier(contract(hidden_t, features, ((1,), (0,))))

    near_up = lax.all_gather(upstream, ("x", "c"), axis=1, tiled=True)
    first = lax.dynamic_slice_in_dim(near_up, jnp.where(early_up, 3, 0) * width, width, 1)
    send(True, 0, product(first))
    up_other = behind(up_other, sent[True, 0][:, : up_other.shape[1]])
    far_up = lax.all_gather(up_other, ("x", "c"), axis=1, tiled=True)
    full_up = jnp.concatenate([near_up, far_up], axis=1)

    def up_block(index):
        at = jnp.bitwise_xor(index, 4 * far_half) * width
        return lax.dynamic_slice_in_dim(full_up, at, width, 1)

    def features_of(pair):
        index = jnp.where(pair >= position, last - pair + position, position - 1 - pair)
        return up_block(jnp.where(early_up, index, last - index))

    parts = {}

    def part_of(pair, after):
        if pair not in parts:
            features = features_of(pair)
            parts[pair] = product(features if after is None else behind(features, sent[after]))
        return parts[pair]

    hg_total = contract(behind(up_block(place), sent[True, 0]), weights, ((1,), (1,)))
    for turn in range(last):
        send(False, turn, part_of(last - 1 - turn, (False, turn - 1) if 0 < turn < last - 1 else (False, 3) if turn else None))
        if turn < last - 1:
            send(True, turn + 1, part_of(turn + 1, (True, turn) if turn else (False, 0)))
        for pair in {turn, last - 1 - turn} if turn >= last // 2 else ():
            block = jnp.where(pair < position, got[True][pair], got[False][last - 1 - pair])
            hg_total = hg_total + contract(features_of(pair), block, ((1,), (1,)))

    own_part = product(behind(up_block(place), sent[False, 4]))
    grads = (own_part + got[True][-1].astype(F32) + got[False][-1].astype(F32)) * scale_hid

    count = (step_index[0] + 1).astype(F32)
    first_new = 0.9 * first_moment + 0.1 * grads
    second_new = 0.999 * second_moment + 0.001 * grads * grads
    correct_one = 1.0 - jnp.power(F32(0.9), count)
    correct_two = 1.0 - jnp.power(F32(0.999), count)
    weights_f = weights.astype(F32)
    step_size = first_new / correct_one / (jnp.sqrt(second_new / correct_two) + 1e-08) + 0.1 * weights_f
    updated = (weights_f - 0.05 * step_size).astype(BF)

    half = updated.shape[0] // 2
    even_step = step_index[0] % 2 == 0
    lower, upper = updated[:half], updated[half:]
    far_sent = lax.optimization_barrier(jnp.where(even_step, upper, lower))
    far = lax.ppermute(far_sent, "y", [(i, (i + 2) % 4) for i in range(4)])
    near_sent = behind(jnp.where(even_step, lower, upper), far_sent)
    near = lax.ppermute(near_sent, "y", [(i, (i + 1) % 4) for i in range(4)])
    partner = jnp.concatenate([jnp.where(even_step, near, far), jnp.where(even_step, far, near)], 0)
    mixed = ((updated.astype(F32) + partner.astype(F32)) * 0.5).astype(BF)

    in_grad = (hg_total * scale_hid).astype(BF)
    return mixed, first_new, second_new, in_grad


def solution(mesh):
    split = Mesh(mesh.devices.reshape(4, LINE, 2, 4, 2), ("y", "zl", "zh", "x", "c"))
    rep, tp = ("y", "zl"), ("zh", "x", "c")
    in_specs = (P(rep, tp), P(rep, tp), P(tp, rep), P(tp, rep), P(tp, rep), P())
    out_specs = (P(tp, rep), P(tp, rep), P(tp, rep), P(rep, tp))
    return jax.shard_map(body, mesh=split, in_specs=in_specs, out_specs=out_specs, check_vma=False)
```

```python
import math

import jax
import jax.numpy as jnp
from jax import lax
from jax.sharding import Mesh, PartitionSpec as P

BF = jnp.bfloat16
F32 = jnp.float32
LINE = 8


def along(value, early):
    pairs = []
    for half in range(2):
        way = 1 if (half == 1) == early else -1
        pairs += [(i * 2 + half, (i + way) * 2 + half) for i in range(LINE) if 0 <= i + way < LINE]
    return lax.ppermute(value, ("zl", "zh"), pairs)


def contract(left, right, dims):
    return lax.dot_general(left, right, (dims, ((), ())), preferred_element_type=F32)


def body(hidden, upstream, weights, first_moment, second_moment, step_index):
    width = weights.shape[1]
    place, far_half = lax.axis_index("zl"), lax.axis_index("zh")
    scale_hid = 1.0 / math.sqrt(7168)

    def behind(value, other):
        return jnp.where(step_index[0] < 0, other, value)

    last = LINE - 1
    early_up = far_half == 1
    position = jnp.where(early_up, place, last - place)

    up_other = lax.ppermute(upstream, "zh", [(0, 1), (1, 0)])
    hidden_t = lax.optimization_barrier(hidden.T)
    got = {True: [along(weights, True)], False: [along(weights, False)]}
    sent = {}

    def send(early, turn, part):
        here = position if early else last - position
        arrived = got[early][-1]
        arrived = behind(arrived, list(sent.values())[-1] if sent else got[not early][-1])
        total = (arrived.astype(F32) + part).astype(BF)
        sent[early, turn] = lax.optimization_barrier(jnp.where(here <= turn, total, arrived))
        got[early].append(along(sent[early, turn], early))

    def product(features):
        return lax.optimization_barrier(contract(hidden_t, features, ((1,), (0,))))

    near_up = lax.all_gather(upstream, ("x", "c"), axis=1, tiled=True)
    first = lax.dynamic_slice_in_dim(near_up, jnp.where(early_up, 3, 0) * width, width, 1)
    send(True, 0, product(first))
    up_other = behind(up_other, sent[True, 0][:, : up_other.shape[1]])
    far_up = lax.all_gather(up_other, ("x", "c"), axis=1, tiled=True)
    full_up = jnp.concatenate([near_up, far_up], axis=1)

    def up_block(index):
        at = jnp.bitwise_xor(index, 4 * far_half) * width
        return lax.dynamic_slice_in_dim(full_up, at, width, 1)

    def features_of(pair):
        index = jnp.where(pair >= position, last - pair + position, position - 1 - pair)
        return up_block(jnp.where(early_up, index, last - index))

    parts = {}

    def part_of(pair, after):
        if pair not in parts:
            features = features_of(pair)
            parts[pair] = product(features if after is None else behind(features, sent[after]))
        return parts[pair]

    hg_total = contract(behind(up_block(place), sent[True, 0]), weights, ((1,), (1,)))
    for turn in range(last):
        send(False, turn, part_of(last - 1 - turn, (False, turn - 1) if 0 < turn < last - 1 else (False, 3) if turn else None))
        if turn < last - 1:
            send(True, turn + 1, part_of(turn + 1, (True, turn) if turn else (False, 0)))
        for pair in {turn, last - 1 - turn} if turn >= last // 2 else ():
            block = jnp.where(pair < position, got[True][pair], got[False][last - 1 - pair])
            hg_total = hg_total + contract(features_of(pair), block, ((1,), (1,)))

    own_part = product(behind(up_block(place), sent[False, 4]))
    grads = (own_part + got[True][-1].astype(F32) + got[False][-1].astype(F32)) * scale_hid

    count = (step_index[0] + 1).astype(F32)
    correct_one = 1.0 - jnp.power(F32(0.9), count)
    correct_two = 1.0 - jnp.power(F32(0.999), count)

    def moments(first, second, grad):
        return 0.9 * first + 0.1 * grad, 0.999 * second + 0.001 * grad * grad

    half = weights.shape[0] // 2
    even_step = step_index[0] % 2 == 0
    near_at = jnp.where(even_step, 0, half)

    def updated_rows(at, after=None):
        first, second, weight, *sums = [
            lax.dynamic_slice_in_dim(x, at, half, 0)
            for x in (first_moment, second_moment, weights, own_part, got[True][-1], got[False][-1])
        ]
        weight = weight if after is None else behind(weight, after)
        grad = (sums[0] + sums[1].astype(F32) + sums[2].astype(F32)) * scale_hid
        first_new, second_new = moments(first, second, grad)
        weight = weight.astype(F32)
        step_size = first_new / correct_one / (jnp.sqrt(second_new / correct_two) + 1e-08) + 0.1 * weight
        return lax.optimization_barrier((weight - 0.05 * step_size).astype(BF))

    def mix(own, partner):
        return ((own.astype(F32) + partner.astype(F32)) * 0.5).astype(BF)

    near_rows = updated_rows(near_at)
    near = lax.ppermute(near_rows, "y", [(i, (i + 1) % 4) for i in range(4)])
    far_rows = updated_rows(half - near_at, near_rows)
    far = lax.ppermute(far_rows, "y", [(i, (i + 2) % 4) for i in range(4)])
    first_new, second_new = moments(first_moment, second_moment, grads)
    near_mixed, far_mixed = mix(near_rows, near), mix(far_rows, far)
    mixed = jnp.concatenate(
        [jnp.where(even_step, near_mixed, far_mixed), jnp.where(even_step, far_mixed, near_mixed)], 0
    )
    in_grad = (hg_total * scale_hid).astype(BF)
    return mixed, first_new, second_new, in_grad


def solution(mesh):
    split = Mesh(mesh.devices.reshape(4, LINE, 2, 4, 2), ("y", "zl", "zh", "x", "c"))
    rep, tp = ("y", "zl"), ("zh", "x", "c")
    in_specs = (P(rep, tp), P(rep, tp), P(tp, rep), P(tp, rep), P(tp, rep), P())
    out_specs = (P(tp, rep), P(tp, rep), P(tp, rep), P(rep, tp))
    return jax.shard_map(body, mesh=split, in_specs=in_specs, out_specs=out_specs, check_vma=False)
```

```python
import math

import jax
import jax.numpy as jnp
from jax import lax
from jax.sharding import Mesh, PartitionSpec as P

BF = jnp.bfloat16
F32 = jnp.float32
LINE = 8


def along(value, early):
    pairs = []
    for half in range(2):
        way = 1 if (half == 1) == early else -1
        pairs += [(i * 2 + half, (i + way) * 2 + half) for i in range(LINE) if 0 <= i + way < LINE]
    return lax.ppermute(value, ("zl", "zh"), pairs)


def contract(left, right, dims):
    return lax.dot_general(left, right, (dims, ((), ())), preferred_element_type=F32)


def body(hidden, upstream, weights, first_moment, second_moment, step_index):
    width = weights.shape[1]
    place, far_half = lax.axis_index("zl"), lax.axis_index("zh")
    scale_hid = 1.0 / math.sqrt(7168)

    def behind(value, other):
        return jnp.where(step_index[0] < 0, other, value)

    last = LINE - 1
    early_up = far_half == 1
    position = jnp.where(early_up, place, last - place)

    up_other = lax.ppermute(upstream, "zh", [(0, 1), (1, 0)])
    hidden_t = lax.optimization_barrier(hidden.T)
    got = {True: [along(weights, True)], False: [along(weights, False)]}
    sent = {}

    def send(early, turn, part):
        here = position if early else last - position
        arrived = got[early][-1]
        arrived = behind(arrived, list(sent.values())[-1] if sent else got[not early][-1])
        total = (arrived.astype(F32) + part).astype(BF)
        sent[early, turn] = lax.optimization_barrier(jnp.where(here <= turn, total, arrived))
        got[early].append(along(sent[early, turn], early))

    def product(features):
        return lax.optimization_barrier(contract(hidden_t, features, ((1,), (0,))))

    near_up = lax.all_gather(upstream, ("x", "c"), axis=1, tiled=True)
    for early in (True, False):
        up_other = behind(up_other, got[early][0][:, : up_other.shape[1]])
    far_up = lax.all_gather(up_other, ("x", "c"), axis=1, tiled=True)
    full_up = jnp.concatenate([near_up, far_up], axis=1)

    def up_block(index):
        at = jnp.bitwise_xor(index, 4 * far_half) * width
        return lax.dynamic_slice_in_dim(full_up, at, width, 1)

    def features_of(pair):
        index = jnp.where(pair >= position, last - pair + position, position - 1 - pair)
        return up_block(jnp.where(early_up, index, last - index))

    parts = {}

    def part_of(pair, after):
        if pair not in parts:
            features = features_of(pair)
            parts[pair] = product(features if after is None else behind(features, sent[after]))
        return parts[pair]

    send(True, 0, part_of(0, None))
    hg_total = contract(behind(up_block(place), sent[True, 0]), weights, ((1,), (1,)))
    for turn in range(last):
        send(False, turn, part_of(last - 1 - turn, (False, turn - 1) if 0 < turn < last - 1 else (False, 3) if turn else None))
        if turn < last - 1:
            send(True, turn + 1, part_of(turn + 1, (True, turn) if turn else (False, 0)))
        for pair in {turn, last - 1 - turn} if turn >= last // 2 else ():
            block = jnp.where(pair < position, got[True][pair], got[False][last - 1 - pair])
            hg_total = hg_total + contract(features_of(pair), block, ((1,), (1,)))

    own_part = product(behind(up_block(place), sent[False, 4]))
    grads = (own_part + got[True][-1].astype(F32) + got[False][-1].astype(F32)) * scale_hid

    count = (step_index[0] + 1).astype(F32)
    correct_one = 1.0 - jnp.power(F32(0.9), count)
    correct_two = 1.0 - jnp.power(F32(0.999), count)

    def moments(first, second, grad):
        return 0.9 * first + 0.1 * grad, 0.999 * second + 0.001 * grad * grad

    half = weights.shape[0] // 2
    even_step = step_index[0] % 2 == 0
    near_at = jnp.where(even_step, 0, half)

    def updated_rows(at, after=None):
        first, second, weight, *sums = [
            lax.dynamic_slice_in_dim(x, at, half, 0)
            for x in (first_moment, second_moment, weights, own_part, got[True][-1], got[False][-1])
        ]
        weight = weight if after is None else behind(weight, after)
        grad = (sums[0] + sums[1].astype(F32) + sums[2].astype(F32)) * scale_hid
        first_new, second_new = moments(first, second, grad)
        weight = weight.astype(F32)
        step_size = first_new / correct_one / (jnp.sqrt(second_new / correct_two) + 1e-08) + 0.1 * weight
        return lax.optimization_barrier((weight - 0.05 * step_size).astype(BF))

    def mix(own, partner):
        return ((own.astype(F32) + partner.astype(F32)) * 0.5).astype(BF)

    near_rows = updated_rows(near_at)
    near = lax.ppermute(near_rows, "y", [(i, (i + 1) % 4) for i in range(4)])
    far_rows = updated_rows(half - near_at, near_rows)
    far = lax.ppermute(far_rows, "y", [(i, (i + 2) % 4) for i in range(4)])
    first_new, second_new = moments(first_moment, second_moment, grads)
    near_mixed, far_mixed = mix(near_rows, near), mix(far_rows, far)
    mixed = jnp.concatenate(
        [jnp.where(even_step, near_mixed, far_mixed), jnp.where(even_step, far_mixed, near_mixed)], 0
    )
    in_grad = (hg_total * scale_hid).astype(BF)
    return mixed, first_new, second_new, in_grad


def solution(mesh):
    split = Mesh(mesh.devices.reshape(4, LINE, 2, 4, 2), ("y", "zl", "zh", "x", "c"))
    rep, tp = ("y", "zl"), ("zh", "x", "c")
    in_specs = (P(rep, tp), P(rep, tp), P(tp, rep), P(tp, rep), P(tp, rep), P())
    out_specs = (P(tp, rep), P(tp, rep), P(tp, rep), P(rep, tp))
    return jax.shard_map(body, mesh=split, in_specs=in_specs, out_specs=out_specs, check_vma=False)
```
